32 devices in a mesh: groups: 2 (over y), wide: 4 (over z), narrow: 4 (over x, core).
Axes of the slice: x: 2, y: 2, z: 4, core: 2. Of those that a mesh axis runs over, the one named last changes fastest.
Arguments:
- tokens: bfloat16 [1024, 16384], P(('groups', 'narrow'), 'wide'), parts along dimension 0, may hold values from -6 to 6
- cotangent: bfloat16 [1024, 16384], P(('groups', 'narrow'), 'wide'), parts along dimension 0, may hold values from -1.5 to 1.5
- gate_weight: bfloat16 [16384, 7168], P('wide', 'narrow'), may hold values from -0.046875 to 0.046875
- up_weight: bfloat16 [16384, 7168], P('wide', 'narrow'), may hold values from -0.046875 to 0.046875
- down_weight: bfloat16 [7168, 16384], P('narrow', 'wide'), may hold values from -0.0625 to 0.0625
Outputs:
- grad_tokens: bfloat16 [1024, 16384], P(('groups', 'narrow'), 'wide'), parts along dimension 0
- grad_gate_weight: bfloat16 [32768, 7168], P(('groups', 'wide'), 'narrow'), parts along dimension 0
- grad_up_weight: bfloat16 [32768, 7168], P(('groups', 'wide'), 'narrow'), parts along dimension 0
- grad_down_weight: bfloat16 [14336, 16384], P(('groups', 'narrow'), 'wide'), parts along dimension 0
The draws below stay inside these ranges and needn't reach their ends.
There are 2 independent parts, one for each index of `groups`. The reference program is written for one: setup_inputs(seed, part) draws one part's arguments, and reference() takes and returns one part's arrays. A program takes and returns all parts, laid end to end along the dimension named above; an argument that names none is the same for every part. Nothing has to cross between parts.
All inputs are finite; a program needn't handle non-finite values.
Results may differ from the reference program's by a relative error of at most 0.0051.
Values may be sent and summed in bfloat16 or wider, within the bound.
A program may use at most 256 MiB of HBM per device.

```python
import jax
import jax.numpy as jnp

D = 16384
FF = 7168
TOKENS = 512


def strengthened(array, rng, source, target, shards_of, factor):
    owner, partner = [(jnp.arange(array.shape[axis_at]) // (array.shape[axis_at] // shards_of)).reshape([-1 if axis == axis_at else 1 for axis in range(array.ndim)]) for axis_at in (source, target)]
    chosen = jax.random.permutation(rng, shards_of)[partner]
    strong = (owner == chosen) | (owner == (partner + shards_of // 2) % shards_of)
    return jnp.where(strong, factor * array, array)


def block_levels(key, shape, cuts, least, largest):
    def one(dim, parts):
        draws = jax.random.uniform(jax.random.fold_in(jax.random.fold_in(key, 6), dim), (parts,), jnp.float32, least / len(cuts), largest / len(cuts))
        return jnp.repeat(jnp.exp(draws), shape[dim] // parts).reshape((-1,) + (1,) * (len(shape) - dim - 1))

    gain = one(*cuts[0])
    for cut in cuts[1:]:
        gain = gain * one(*cut)
    return gain


def centred(stream_key, shape, deviation, reach, shards=(), kind=jnp.bfloat16):
    values = jax.random.normal(stream_key, shape, jnp.float32) * deviation
    if len(shards) > 0:
        values = block_levels(stream_key, shape, shards, -0.22, 0.18) * values
    return jnp.clip(values, min=-reach, max=reach).astype(kind)


def bell_draw_with(stream_key, shape, spread, limit, pieces, heavy, kind=jnp.bfloat16):
    drawn = spread * jax.random.normal(stream_key, shape, jnp.float32)
    if pieces:
        drawn = drawn * block_levels(stream_key, shape, pieces, -0.22, 0.18)
    return jnp.clip(strengthened(drawn, jax.random.fold_in(stream_key, 3), *heavy), -limit, limit).astype(kind)


def setup_inputs(seed: int = 0, part: int = 0) -> dict:
    key_of = jax.random.split(jax.random.key(seed), 6)
    part_splits = jax.random.split(jax.random.fold_in(key_of[5], part), 6)
    tokens = bell_draw_with(part_splits[0], (TOKENS, D), 1.0, 6.0, ((0, 4), (1, 4)), (1, 0, 4, 2.0))
    cotangent = bell_draw_with(part_splits[1], (TOKENS, D), 0.25, 1.5, ((0, 4), (1, 4)), (1, 0, 4, 2.0))
    gate_weight = centred(key_of[2], (D, FF), D ** -0.5, 0.046875, ((0, 4), (1, 4)))
    up_weight = centred(key_of[3], (D, FF), D ** -0.5, 0.046875, ((0, 4), (1, 4)))
    down_weight = centred(key_of[4], (FF, D), FF ** -0.5, 0.0625, ((0, 4), (1, 4)))
    return {"tokens": tokens, "cotangent": cotangent, "gate_weight": gate_weight, "up_weight": up_weight, "down_weight": down_weight}


def reference(tokens, cotangent, gate_weight, up_weight, down_weight):
    gate_pre = jnp.dot(tokens, gate_weight, preferred_element_type=jnp.float32)
    up_pre = jnp.dot(tokens, up_weight, preferred_element_type=jnp.float32)
    grad_hidden = jnp.dot(cotangent, down_weight.T, preferred_element_type=jnp.float32)
    sig_gate = jax.nn.sigmoid(gate_pre)
    act_gate = gate_pre * sig_gate
    hidden = (act_gate * up_pre).astype(jnp.bfloat16)
    grad_gate = (grad_hidden * up_pre * sig_gate * (1.0 + gate_pre * (1.0 - sig_gate))).astype(jnp.bfloat16)
    grad_up = (grad_hidden * act_gate).astype(jnp.bfloat16)
    grad_down = jnp.dot(hidden.T, cotangent, preferred_element_type=jnp.float32).astype(jnp.bfloat16)
    grad_gw = jnp.dot(tokens.T, grad_gate, preferred_element_type=jnp.float32).astype(jnp.bfloat16)
    grad_uw = jnp.dot(tokens.T, grad_up, preferred_element_type=jnp.float32).astype(jnp.bfloat16)
    grad_input = jnp.dot(grad_gate, gate_weight.T, preferred_element_type=jnp.float32)
    grad_input = grad_input + jnp.dot(grad_up, up_weight.T, preferred_element_type=jnp.float32)
    return grad_input.astype(jnp.bfloat16), grad_gw, grad_uw, grad_down
```

```python
import math

import jax
import jax.numpy as jnp
from jax import lax
from jax.experimental import pallas as pl
from jax.experimental.pallas import tpu as pltpu
from jax.sharding import PartitionSpec as P

PIECES = 2


def swiglu_backward(gate_pre, up_pre, grad_hidden):
    sig_gate = jax.nn.sigmoid(gate_pre)
    act_gate = gate_pre * sig_gate
    hidden = (act_gate * up_pre).astype(jnp.bfloat16)
    grad_gate = (grad_hidden * up_pre * sig_gate * (1.0 + gate_pre * (1.0 - sig_gate))).astype(
        jnp.bfloat16
    )
    grad_up = (grad_hidden * act_gate).astype(jnp.bfloat16)
    return (hidden, grad_gate, grad_up)


def contract_rows(left_mat, right_mat):
    return lax.dot_general(
        left_mat, right_mat, (((0,), (0,)), ((), ())), preferred_element_type=jnp.float32
    )


def contract_cols(left_mat, right_mat):
    return lax.dot_general(
        left_mat, right_mat, (((1,), (1,)), ((), ())), preferred_element_type=jnp.float32
    )


def power_below(bound):
    return 2.0 ** math.floor(math.log2(65000.0 / bound))


def block_of(size, most):
    return max(b for b in range(128, most + 1, 128) if size % b == 0)


def weight_gradients(left_mat, rights, most):
    count, (depth, rows) = len(rights), left_mat.shape
    block = block_of(rows, most)

    def kernel(left_ref, *refs):
        left = left_ref[...].T
        for right_ref, out_ref in zip(refs[:count], refs[count:]):
            out_ref[...] = jnp.dot(
                left, right_ref[...], preferred_element_type=jnp.float32
            ).astype(jnp.bfloat16)

    wide = [r.shape[1] for r in rights]
    return pl.pallas_call(
        kernel,
        grid=(rows // block,),
        in_specs=[pl.BlockSpec((depth, block), lambda i: (0, i))]
        + [pl.BlockSpec((depth, w), lambda i: (0, 0)) for w in wide],
        out_specs=[pl.BlockSpec((block, w), lambda i: (i, 0)) for w in wide],
        out_shape=[jax.ShapeDtypeStruct((rows, w), jnp.bfloat16) for w in wide],
        compiler_params=pltpu.CompilerParams(vmem_limit_bytes=48 * 2**20),
        cost_estimate=pl.CostEstimate(
            flops=2 * depth * rows * sum(wide),
            bytes_accessed=2 * (depth * rows + (depth + rows) * sum(wide)),
            transcendentals=0,
        ),
    )(left_mat, *rights)


def input_gradient(grad_gate, grad_up, gate_weight, up_weight):
    (rows, hid), depth = grad_gate.shape, gate_weight.shape[0]
    block = block_of(depth, 512)

    def kernel(gate_ref, up_ref, gate_weight_ref, up_weight_ref, out_ref):
        total = contract_cols(gate_ref[...], gate_weight_ref[...])
        out_ref[...] = (total + contract_cols(up_ref[...], up_weight_ref[...])).astype(
            jnp.bfloat16
        )

    held = pl.BlockSpec((rows, hid), lambda i: (0, 0))
    streamed = pl.BlockSpec((block, hid), lambda i: (i, 0))
    return pl.pallas_call(
        kernel,
        grid=(depth // block,),
        in_specs=[held, held, streamed, streamed],
        out_specs=pl.BlockSpec((rows, block), lambda i: (0, i)),
        out_shape=jax.ShapeDtypeStruct((rows, depth), jnp.bfloat16),
        compiler_params=pltpu.CompilerParams(vmem_limit_bytes=48 * 2**20),
        cost_estimate=pl.CostEstimate(
            flops=4 * depth * rows * hid,
            bytes_accessed=4 * (depth * hid + rows * hid) + 2 * rows * depth,
            transcendentals=0,
        ),
    )(grad_gate, grad_up, gate_weight, up_weight)


def on_device(tokens, cotangent, gate_weight, up_weight, down_weight):
    n_narrow, n_wide = lax.axis_size("narrow"), lax.axis_size("wide")
    chips = n_narrow // 2
    rows, depth = tokens.shape
    hid = gate_weight.shape[1]
    width = hid // PIECES
    up_scale = power_below(6.0 * 0.046875 * depth * n_wide)
    back_scale = power_below(1.5 * 0.0625 * depth * n_wide)
    swap = [(i, i ^ 1) for i in range(n_narrow)]
    core = lax.axis_index("narrow") % 2
    place = lax.axis_index("wide")

    def from_chip(array, k):
        pairs = [(i, (i + 2 * k) % n_narrow) for i in range(n_narrow)]
        return lax.ppermute(array, "narrow", pairs) if k else array

    def hop_pairs(block, hop):
        pairs = []
        for i in range(n_narrow):
            rightward = (block + i % 2) % 2 == 0
            src, dst = (hop, hop + 1) if rightward else (n_wide - 1 - hop, n_wide - 2 - hop)
            pairs.append((src * n_narrow + i, dst * n_narrow + i))
        return pairs

    def reversed_pairs(pairs):
        return [(b, a) for a, b in pairs]

    def move(array, pairs):
        return lax.ppermute(array, ("wide", "narrow"), pairs)

    def add(own, other):
        return own.astype(jnp.float32) + other.astype(jnp.float32)

    tok_far = [from_chip(tokens, k) for k in range(chips)]
    cot_far = [from_chip(cotangent, k) for k in range(chips)]

    owns, sents, hops, totals = {}, {}, {}, {}

    def advance(chain):
        hop = hops[chain]
        totals[chain] = add(owns[chain], move(sents[chain], hop_pairs(chain[0], hop)))
        sents[chain] = totals[chain].astype(jnp.float16)
        hops[chain] = hop + 1

    tok_blocks, cot_blocks = [], []
    for k in range(chips):
        tok, cot = tok_far[k], cot_far[k]
        if k:
            first = (k - 1, 0)
            advance(first)
            tok, cot, sents[first] = lax.optimization_barrier((tok, cot, sents[first]))
        tok = jnp.concatenate([tok, lax.ppermute(tok, "narrow", swap)], axis=0)
        cot = jnp.concatenate([cot, lax.ppermute(cot, "narrow", swap)], axis=0)
        tok_blocks.append(tok)
        cot_blocks.append(cot)
        gate_part = jnp.dot(tok, gate_weight, preferred_element_type=jnp.float32)
        up_part = jnp.dot(tok, up_weight, preferred_element_type=jnp.float32)
        if k:
            before = [(k - 1, j) for j in range(PIECES)]
            for chain in before:
                advance(chain)
            cot, *states = lax.optimization_barrier((cot, *(sents[c] for c in before)))
            sents.update(zip(before, states))
        back_part = contract_cols(cot, down_weight)
        parts = (
            (gate_part * up_scale).astype(jnp.float16),
            (up_part * up_scale).astype(jnp.float16),
            (back_part * back_scale).astype(jnp.float16),
        )
        for j in range(PIECES):
            owns[k, j] = sents[k, j] = jnp.concatenate(
                [p[:, j * width : (j + 1) * width] for p in parts], axis=1
            )
            hops[k, j] = 0

    hid_blocks, gate_blocks, up_blocks = [], [], []
    for k in range(chips):
        pieces = []
        for j in range(PIECES):
            while hops[k, j] < n_wide - 1:
                advance((k, j))
            total = totals[k, j]
            values = swiglu_backward(
                total[:, :width] * (1.0 / up_scale),
                total[:, width : 2 * width] * (1.0 / up_scale),
                total[:, 2 * width :] * (1.0 / back_scale),
            )
            value = jnp.concatenate(values, axis=1)
            rightward = (k + core) % 2 == 0
            from_end = jnp.where(rightward, n_wide - 1 - place, place)
            result = value
            for hop in reversed(range(n_wide - 1)):
                value = move(value, reversed_pairs(hop_pairs(k, hop)))
                result = jnp.where(from_end == n_wide - 1 - hop, value, result)
            pieces.append(result)
        for n, blocks in enumerate((hid_blocks, gate_blocks, up_blocks)):
            blocks.append(
                jnp.concatenate([p[:, n * width : (n + 1) * width] for p in pieces], axis=1)
            )

    grad_input = None
    for k in reversed(range(chips)):
        part = input_gradient(gate_blocks[k], up_blocks[k], gate_weight, up_weight)
        other = lax.ppermute(part[rows:], "narrow", swap)
        part = add(part[:rows], other)
        if k:
            part = from_chip(part.astype(jnp.bfloat16), chips - k)
        part = part.astype(jnp.float32)
        grad_input = part if grad_input is None else grad_input + part

    tok_full = jnp.concatenate(tok_blocks, axis=0)
    cot_full = jnp.concatenate(cot_blocks, axis=0)
    grad_gw, grad_uw = weight_gradients(
        tok_full, [jnp.concatenate(b, axis=0) for b in (gate_blocks, up_blocks)], 512
    )
    (grad_down,) = weight_gradients(jnp.concatenate(hid_blocks, axis=0), [cot_full], 256)
    return (grad_input.astype(jnp.bfloat16), grad_gw, grad_uw, grad_down)


def solution(mesh):
    return jax.shard_map(
        on_device,
        mesh=mesh,
        in_specs=(
            P(("groups", "narrow"), "wide"),
            P(("groups", "narrow"), "wide"),
            P("wide", "narrow"),
            P("wide", "narrow"),
            P("narrow", "wide"),
        ),
        out_specs=(
            P(("groups", "narrow"), "wide"),
            P(("groups", "wide"), "narrow"),
            P(("groups", "wide"), "narrow"),
            P(("groups", "narrow"), "wide"),
        ),
        check_vma=False,
    )
```

```python
import math

import jax
import jax.numpy as jnp
from jax import lax
from jax.experimental import pallas as pl
from jax.experimental.pallas import tpu as pltpu
from jax.sharding import PartitionSpec as P

PIECES = 4


def swiglu_backward(gate_pre, up_pre, grad_hidden):
    sig_gate = jax.nn.sigmoid(gate_pre)
    act_gate = gate_pre * sig_gate
    hidden = (act_gate * up_pre).astype(jnp.bfloat16)
    grad_gate = (grad_hidden * up_pre * sig_gate * (1.0 + gate_pre * (1.0 - sig_gate))).astype(
        jnp.bfloat16
    )
    grad_up = (grad_hidden * act_gate).astype(jnp.bfloat16)
    return (hidden, grad_gate, grad_up)


def contract_rows(left_mat, right_mat):
    return lax.dot_general(
        left_mat, right_mat, (((0,), (0,)), ((), ())), preferred_element_type=jnp.float32
    )


def contract_cols(left_mat, right_mat):
    return lax.dot_general(
        left_mat, right_mat, (((1,), (1,)), ((), ())), preferred_element_type=jnp.float32
    )


def power_below(bound):
    return 2.0 ** math.floor(math.log2(65000.0 / bound))


def block_of(size, most):
    return max(b for b in range(128, most + 1, 128) if size % b == 0)


def weight_gradients(left_mat, rights, most):
    count, (depth, rows) = len(rights), left_mat.shape
    block = block_of(rows, most)

    def kernel(left_ref, *refs):
        left = left_ref[...].T
        for right_ref, out_ref in zip(refs[:count], refs[count:]):
            out_ref[...] = jnp.dot(
                left, right_ref[...], preferred_element_type=jnp.float32
            ).astype(jnp.bfloat16)

    wide = [r.shape[1] for r in rights]
    return pl.pallas_call(
        kernel,
        grid=(rows // block,),
        in_specs=[pl.BlockSpec((depth, block), lambda i: (0, i))]
        + [pl.BlockSpec((depth, w), lambda i: (0, 0)) for w in wide],
        out_specs=[pl.BlockSpec((block, w), lambda i: (i, 0)) for w in wide],
        out_shape=[jax.ShapeDtypeStruct((rows, w), jnp.bfloat16) for w in wide],
        compiler_params=pltpu.CompilerParams(vmem_limit_bytes=48 * 2**20),
        cost_estimate=pl.CostEstimate(
            flops=2 * depth * rows * sum(wide),
            bytes_accessed=2 * (depth * rows + (depth + rows) * sum(wide)),
            transcendentals=0,
        ),
    )(left_mat, *rights)


def input_gradient(grad_gate, grad_up, gate_weight, up_weight):
    (rows, hid), depth = grad_gate.shape, gate_weight.shape[0]
    block = block_of(depth, 512)

    def kernel(gate_ref, up_ref, gate_weight_ref, up_weight_ref, out_ref):
        total = contract_cols(gate_ref[...], gate_weight_ref[...])
        out_ref[...] = (total + contract_cols(up_ref[...], up_weight_ref[...])).astype(
            jnp.bfloat16
        )

    held = pl.BlockSpec((rows, hid), lambda i: (0, 0))
    streamed = pl.BlockSpec((block, hid), lambda i: (i, 0))
    return pl.pallas_call(
        kernel,
        grid=(depth // block,),
        in_specs=[held, held, streamed, streamed],
        out_specs=pl.BlockSpec((rows, block), lambda i: (0, i)),
        out_shape=jax.ShapeDtypeStruct((rows, depth), jnp.bfloat16),
        compiler_params=pltpu.CompilerParams(vmem_limit_bytes=48 * 2**20),
        cost_estimate=pl.CostEstimate(
            flops=4 * depth * rows * hid,
            bytes_accessed=4 * (depth * hid + rows * hid) + 2 * rows * depth,
            transcendentals=0,
        ),
    )(grad_gate, grad_up, gate_weight, up_weight)


def on_device(tokens, cotangent, gate_weight, up_weight, down_weight):
    n_narrow, n_wide = lax.axis_size("narrow"), lax.axis_size("wide")
    chips = n_narrow // 2
    rows, depth = tokens.shape
    hid = gate_weight.shape[1]
    piece = 2 * rows // PIECES
    steps = PIECES + n_wide - 2
    up_scale = power_below(6.0 * 0.046875 * depth * n_wide)
    back_scale = power_below(1.5 * 0.0625 * depth * n_wide)
    swap = [(i, i ^ 1) for i in range(n_narrow)]
    core = lax.axis_index("narrow") % 2
    place = lax.axis_index("wide")

    def from_chip(array, k):
        pairs = [(i, (i + 2 * k) % n_narrow) for i in range(n_narrow)]
        return lax.ppermute(array, "narrow", pairs) if k else array

    def along(block):
        return jnp.where((block + core) % 2 == 0, place, n_wide - 1 - place)

    def line_pairs(block, step, back):
        pairs = []
        for i in range(n_narrow):
            rightward = (block + i % 2) % 2 == 0
            for at in range(n_wide - 1):
                if 0 <= step - at < PIECES:
                    src, dst = (n_wide - 1 - at, n_wide - 2 - at) if back else (at, at + 1)
                    if not rightward:
                        src, dst = n_wide - 1 - src, n_wide - 1 - dst
                    pairs.append((src * n_narrow + i, dst * n_narrow + i))
        return pairs

    def move(array, pairs):
        return lax.ppermute(array, ("wide", "narrow"), pairs)

    def add(own, other):
        return own.astype(jnp.float32) + other.astype(jnp.float32)

    tok_far = [from_chip(tokens, k) for k in range(chips)]
    cot_far = [from_chip(cotangent, k) for k in range(chips)]

    owns, sums = {}, {}

    def advance(k):
        step = len(sums[k])
        at = jnp.clip(step - along(k), 0, PIECES - 1) * piece
        total = lax.dynamic_slice_in_dim(owns[k], at, piece, axis=0).astype(jnp.float32)
        if step:
            sent = sums[k][-1].astype(jnp.float16)
            total = total + move(sent, line_pairs(k, step - 1, False)).astype(jnp.float32)
        sums[k].append(total)

    def behind(array, k, count):
        if k < 0:
            return array
        for _ in range(count):
            advance(k)
        array, sums[k][-1] = lax.optimization_barrier((array, sums[k][-1]))
        return array

    tok_blocks, cot_blocks = [], []
    for k in range(chips):
        tok, cot = tok_far[k], cot_far[k]
        if k:
            tok, cot, _ = lax.optimization_barrier((tok, cot, owns[k - 1]))
        tok = jnp.concatenate([tok, lax.ppermute(tok, "narrow", swap)], axis=0)
        cot = jnp.concatenate([cot, lax.ppermute(cot, "narrow", swap)], axis=0)
        tok_blocks.append(tok)
        cot_blocks.append(cot)
        tok = behind(tok, k - 1, 2)
        gate_part = jnp.dot(tok, gate_weight, preferred_element_type=jnp.float32)
        tok = behind(tok, k - 1, 1)
        up_part = jnp.dot(tok, up_weight, preferred_element_type=jnp.float32)
        cot = behind(cot, k - 1, 1)
        back_part = contract_cols(cot, down_weight)
        parts = (
            (gate_part * up_scale).astype(jnp.float16),
            (up_part * up_scale).astype(jnp.float16),
            (back_part * back_scale).astype(jnp.float16),
        )
        owns[k] = jnp.concatenate(parts, axis=1)
        sums[k] = []

    hid_blocks, gate_blocks, up_blocks = [], [], []
    for k in range(chips):
        while len(sums[k]) < steps + 1:
            advance(k)
        to_end = n_wide - 1 - along(k)
        held = []
        for step in range(steps + 1):
            if step:
                value = move(held[-1], line_pairs(k, step - 1, True))
            if step < PIECES:
                total = sums[k][step + n_wide - 1]
                result = swiglu_backward(
                    total[:, :hid] * (1.0 / up_scale),
                    total[:, hid : 2 * hid] * (1.0 / up_scale),
                    total[:, 2 * hid :] * (1.0 / back_scale),
                )
                result = jnp.concatenate(result, axis=1)
                value = jnp.where(to_end == 0, result, value) if step else result
            held.append(value)
        whole = lax.dynamic_slice_in_dim(
            jnp.concatenate(held, axis=0), to_end * piece, 2 * rows, axis=0
        )
        for n, blocks in enumerate((hid_blocks, gate_blocks, up_blocks)):
            blocks.append(whole[:, n * hid : (n + 1) * hid])

    hid_all, gate_all, up_all = (
        jnp.concatenate(b, axis=0) for b in (hid_blocks, gate_blocks, up_blocks)
    )
    grad_tokens = input_gradient(gate_all, up_all, gate_weight, up_weight)
    parts = [grad_tokens[2 * k * rows : 2 * (k + 1) * rows] for k in range(chips)]
    grad_input = None
    for k in reversed(range(chips)):
        part = add(parts[k][:rows], lax.ppermute(parts[k][rows:], "narrow", swap))
        if k:
            part = from_chip(part.astype(jnp.bfloat16), chips - k)
        part = part.astype(jnp.float32)
        grad_input = part if grad_input is None else grad_input + part

    tok_full = jnp.concatenate(tok_blocks, axis=0)
    cot_full = jnp.concatenate(cot_blocks, axis=0)
    grad_gw, grad_uw = weight_gradients(
        tok_full, [gate_all, up_all], 512
    )
    (grad_down,) = weight_gradients(hid_all, [cot_full], 256)
    return (grad_input.astype(jnp.bfloat16), grad_gw, grad_uw, grad_down)


def solution(mesh):
    return jax.shard_map(
        on_device,
        mesh=mesh,
        in_specs=(
            P(("groups", "narrow"), "wide"),
            P(("groups", "narrow"), "wide"),
            P("wide", "narrow"),
            P("wide", "narrow"),
            P("narrow", "wide"),
        ),
        out_specs=(
            P(("groups", "narrow"), "wide"),
            P(("groups", "wide"), "narrow"),
            P(("groups", "wide"), "narrow"),
            P(("groups", "narrow"), "wide"),
        ),
        check_vma=False,
    )
```
